128 devices in a mesh: dp: 8 (over y_lo, x), tensor: 16 (over y_hi, z, core).
Axes of the slice: x: 4, y: 4 (y_hi: 2, y_lo: 2; y = y_hi * 2 + y_lo), z: 4, core: 2. Of those that a mesh axis runs over, the one named last changes fastest.
Arguments:
- gradient: bfloat16 [8, 4096, 14336], P('dp', None, 'tensor'), may hold values from -45 to 45
- error_in: bfloat16 [8, 4096, 14336], P('dp', None, 'tensor'), may hold values from -3 to 3
- warm_start: float32 [64, 14336], P(None, 'tensor'), may hold values from -6 to 6
Outputs:
- right_factor: float32 [64, 14336], P(None, 'tensor')
- error_out: bfloat16 [8, 4096, 14336], P('dp', None, 'tensor')
The draws below stay inside these ranges and needn't reach their ends.
All inputs are finite; a program needn't handle non-finite values.
Results may differ from the reference program's by a relative error of at most 0.001.
Values sent between devices are 32-bit elements; how exact they have to be, the bound alone decides.
A program may use at most 128 MiB of HBM per device.

```python
import math
import jax
import jax.numpy as jnp
from jax import lax

D = 4096
FF = 14336
R = 64
ITERS = 4
REPL = 8


def draw_gradient(key, part):
    key = jax.random.fold_in(key, 1)
    key_base, key_rows, key_cols = jax.random.split(key, 3)
    base = jnp.clip(jax.random.normal(key_base, (REPL, D, FF), jnp.float32), -4.0, 4.0)
    low, high = (math.log(0.3), math.log(3.0))
    rows = jnp.exp(jax.random.uniform(key_rows, (REPL, D, 1), jnp.float32, low, high))
    cols = jnp.exp(jax.random.uniform(key_cols, (REPL, 1, FF), jnp.float32, low, high))
    return (base * rows * cols).astype(jnp.bfloat16)


def block_levels(key, extent, cuts, least, largest):
    loudness, own = 1.0, jax.random.fold_in(key, 6)
    for dim, shards_of in cuts:
        draws = jnp.exp(jax.random.uniform(jax.random.fold_in(own, dim), (shards_of,), jnp.float32, least / len(cuts), largest / len(cuts)))
        loudness = loudness * jnp.repeat(draws, extent[dim] // shards_of).reshape([-1 if axis == dim else 1 for axis in range(len(extent))])
    return loudness


def noise(rng, shape, deviation, limit, shards=(), kind=jnp.bfloat16):
    level = block_levels(rng, shape, shards, -0.22, 0.18) if shards else 1.0
    entries = jax.random.normal(rng, shape, jnp.float32) * deviation * level
    return jnp.minimum(jnp.maximum(entries, -limit), limit).astype(kind)


def setup_inputs(seed: int = 0) -> dict:
    streams_of = jax.random.split(jax.random.key(seed), 4)
    return {
        "gradient": draw_gradient(jax.random.fold_in(streams_of[3], 71), 0),
        "error_in": noise(streams_of[1], (REPL, D, FF), 0.5, 3.0, ((0, 8), (2, 16))),
        "warm_start": noise(streams_of[2], (R, FF), 1.0, 6.0, ((1, 16),), jnp.float32),
    }


def orthonormal(left):
    for sweep in range(2):
        gram_matrix = jnp.dot(left, left.T, precision=lax.Precision.HIGHEST)
        factor = jnp.linalg.cholesky(gram_matrix)
        left = lax.linalg.triangular_solve(factor, left, left_side=True, lower=True)
    return left

def reference(gradient, error_in, warm_start):

    def merged_of(index):
        grad_row = lax.dynamic_index_in_dim(gradient, index, 0, keepdims=False)
        err_row = lax.dynamic_index_in_dim(error_in, index, 0, keepdims=False)
        return grad_row.astype(jnp.float32) + err_row.astype(jnp.float32)
    right = warm_start
    basis = jnp.zeros((R, D), jnp.float32)
    for sweep in range(ITERS):

        def left_step(index, total):
            merged = merged_of(index)
            return total + lax.dot_general(right.astype(jnp.float32), merged.astype(jnp.float32), (((1,), (1,)), ((), ())), precision=lax.Precision.HIGHEST, preferred_element_type=jnp.float32)
        left = lax.fori_loop(0, REPL, left_step, jnp.zeros((R, D), jnp.float32))
        basis = orthonormal(left)

        def right_step(index, total):
            merged = merged_of(index)
            return total + jnp.dot(basis, merged, precision=lax.Precision.HIGHEST)
        right = lax.fori_loop(0, REPL, right_step, jnp.zeros((R, FF), jnp.float32)) / REPL
    approx = jnp.dot(basis.T, right, precision=lax.Precision.HIGHEST)

    def new_error(index):
        return (merged_of(index) - approx).astype(jnp.bfloat16)
    error_out = lax.map(new_error, jnp.arange(REPL, dtype=jnp.int32))
    return (right, error_out)
```

```python
import jax
import jax.numpy as jnp
from jax import lax
from jax.experimental import pallas as pl
from jax.experimental.pallas import tpu as pltpu
from jax.sharding import PartitionSpec as P

ITERS = 4
REPL = 8
R = 64
D = 4096
COLS = 896
CHUNKS = 4
ROWS = D // CHUNKS
PIECE = 16
BLOCK = 512
MESH = pl.DeviceIdType.MESH
F32 = jnp.float32
BF16 = jnp.bfloat16
HIGHEST = lax.Precision.HIGHEST


def hops(step):
    return min(step, 4 - step)


OFFSETS = sorted(
    [(i, j, k) for i in range(4) for j in range(4) for k in range(4) if i + j + k],
    key=lambda o: -sum(map(hops, o)),
)


def terms(value):
    high = value.astype(BF16)
    rest = value - high.astype(F32)
    middle = rest.astype(BF16)
    low = (rest - middle.astype(F32)).astype(BF16)
    return high, middle, low


def sum_terms(product):
    return product[0:R] + product[R : 2 * R] + product[2 * R : 3 * R]


def contract(a, b, dim_a, dim_b, precision=None):
    return lax.dot_general(
        a, b, (((dim_a,), (dim_b,)), ((), ())), precision=precision, preferred_element_type=F32
    )


def inverse_cholesky(gram):
    ahead = 8
    lane = lax.broadcasted_iota(jnp.int32, (R, 2 * R), 1)
    sub = lax.broadcasted_iota(jnp.int32, (R, 2 * R), 0)
    work = jnp.concatenate([gram, jnp.zeros((R, R), F32)], axis=1)
    work = jnp.where(lane == sub + R, 1.0, work)
    for j in range(0, R, ahead):
        cols = [jnp.broadcast_to(work[:, j + k : j + k + 1], (R, 2 * R)) for k in range(ahead)]
        rows = [work[j + k : j + k + 1, :] for k in range(ahead)]
        factors = []
        for k in range(ahead):
            pivot = 1.0 / cols[k][j + k : j + k + 1, :]
            factor = jnp.where(sub > j + k, cols[k] * pivot, 0.0)
            factors.append(factor)
            for m in range(k + 1, ahead):
                cols[m] = cols[m] - factor * cols[m][j + k : j + k + 1, :]
                rows[m] = rows[m] - factor[j + m : j + m + 1, :] * rows[k]
        for k in range(ahead):
            work = work - factors[k] * rows[k]
    diagonal = jnp.sum(jnp.where(lane == sub, work, 0.0), axis=1, keepdims=True)
    return work[:, R:] * lax.rsqrt(diagonal)


def kernel(
    gradient, error, warm, right_out, error_out,
    both, rr, part, cross, mine, slots, left, flat, raw_part, raw_slots, raw, basis_terms, stage,
    load_sem, cross_send, cross_recv, rs_send, rs_recv, ag_send, ag_recv, fwd_send, fwd_recv,
    dp_send, dp_recv, dpg_send, dpg_recv, out_sem,
):
    d, t = lax.axis_index("dp"), lax.axis_index("tensor")
    x, y, z, c = d % 4, (t // 8) * 2 + d // 4, (t // 2) % 4, t % 2
    other = 1 - c
    group = (x + y + z) % 4
    place = x * 4 + y
    chip = place * 4 + z
    own = group * 32 + c * 16 + place

    def device(i, j, k):
        return ((j % 2) * 4 + i, (j // 2) * 8 + k * 2 + c)

    def away(o):
        return device((x + o[0]) % 4, (y + o[1]) % 4, (z + o[2]) % 4)

    sibling = (d, (t // 2) * 2 + other)

    def load(j):
        rows = pl.ds(j * ROWS, ROWS)
        return (
            pltpu.make_async_copy(gradient.at[0, rows], both.at[rows, 0:COLS], load_sem.at[j, 0]),
            pltpu.make_async_copy(error.at[0, rows], both.at[rows, COLS : 2 * COLS], load_sem.at[j, 1]),
        )

    for j in range(CHUNKS):
        for copy in load(j):
            copy.start()

    barrier = pltpu.get_barrier_semaphore()
    for o in OFFSETS:
        pl.semaphore_signal(barrier, 1, device_id=away(o), device_id_type=MESH)
    pl.semaphore_signal(barrier, 1, device_id=sibling, device_id_type=MESH)

    def set_right(value):
        for i, term in enumerate(terms(value)):
            rr[i * R : (i + 1) * R, 0:COLS] = term
            rr[i * R : (i + 1) * R, COLS : 2 * COLS] = term

    set_right(warm[...])
    pl.semaphore_wait(barrier, len(OFFSETS) + 1)

    def remote(src, dst, send, recv, target):
        return pltpu.make_async_remote_copy(src, dst, send, recv, device_id=target, device_id_type=MESH)

    def cross_copy(j):
        return remote(part.at[pl.ds(j * 32 + other * 16, 16)], cross.at[j], cross_send.at[j], cross_recv.at[j], sibling)

    def fwd_copy(j):
        half = left.at[pl.ds(j * 32 + c * 16, 16)]
        return remote(half, half, fwd_send.at[j], fwd_recv.at[j], sibling)

    def left_chunk(j):
        rows = pl.ds(pl.multiple_of(j * ROWS, ROWS), ROWS)
        product = sum_terms(contract(rr[...], both[rows, :], 1, 1))
        for b in range(8):
            part[pl.ds(j * 32 + b * 4, 4)] = product[:, b * 128 : (b + 1) * 128].reshape(4, PIECE, 128)
        cross_copy(j).start()

    def scatter_chunk(j):
        cross_copy(j).wait_recv()
        mine[j] = part[pl.ds(j * 32 + c * 16, 16)] + cross[j]
        for r in (10, 2, 8, 6, 14, 9, 11, 5, 7, 13, 15, 1, 3, 4, 12, 0):
            i, k = (x + r // 4) % 4, (y + r % 4) % 4
            copy = remote(mine.at[j, i * 4 + k], slots.at[chip], rs_send, rs_recv, device(i, k, (j - i - k + 8) % 4))
            if r:
                copy.start()
            else:

                @pl.when(j != group)
                def _():
                    copy.start()

                @pl.when(j == group)
                def _():
                    slots[chip] = mine[j, place]

    def right_chunk(j, gram):
        @pl.when(j == group)
        def _():
            remote(left.at[0:15], left.at[0:15], ag_send, ag_recv.at[j], sibling).wait_recv()

        @pl.when(j != group)
        def _():
            remote(left.at[0:16], left.at[0:16], ag_send, ag_recv.at[j], sibling).wait_recv()

        fwd_copy(j).start()
        fwd_copy(j).wait_recv()
        rows = pl.ds(pl.multiple_of(j * ROWS, ROWS), ROWS)
        blocks = left[pl.ds(j * 32, 32)].reshape(8, R, 128)
        value = jnp.concatenate([blocks[b] for b in range(8)], axis=1)
        flat[:, rows] = value
        stacked = jnp.concatenate(terms(value), axis=0)
        product = sum_terms(contract(stacked, both[rows, :], 1, 0))
        raw_part[...] += product[:, 0:COLS] + product[:, COLS : 2 * COLS]
        return gram + contract(value, value, 1, 1, HIGHEST)

    def ranks(owner):
        return pl.ds(pl.multiple_of(owner * 8, 8), 8)

    def iteration(step, _):
        def left_step(j, carry):
            @pl.when(step == 0)
            def _():
                rows = pl.ds(pl.multiple_of(j * ROWS, ROWS), ROWS)
                pltpu.make_async_copy(gradient.at[0, rows], both.at[rows, 0:COLS], load_sem.at[j, 0]).wait()
                pltpu.make_async_copy(error.at[0, rows], both.at[rows, COLS : 2 * COLS], load_sem.at[j, 1]).wait()

            left_chunk(j)

            @pl.when(j > 0)
            def _():
                scatter_chunk(j - 1)

            return carry

        lax.fori_loop(0, CHUNKS, left_step, 0)
        scatter_chunk(CHUNKS - 1)
        raw_part[...] = jnp.zeros_like(raw_part)
        remote(slots.at[0:63], slots.at[0:63], rs_send, rs_recv, sibling).wait_recv()
        left[own] = jnp.sum(slots[...], axis=0)
        for o in OFFSETS:
            remote(left.at[own], left.at[own], ag_send, ag_recv.at[group], away(o)).start()

        gram = lax.fori_loop(0, CHUNKS, right_chunk, jnp.zeros((R, R), F32))

        def dp_device(k):
            return lax.rem(d + k, REPL)

        for k in (6, 2, 5, 7, 1, 3, 4):
            owner = dp_device(k)
            remote(raw_part.at[ranks(owner)], raw_slots.at[d], dp_send, dp_recv, (owner, t)).start()
        raw_slots[d] = raw_part[ranks(d)]

        first = inverse_cholesky(gram)
        left_one = jnp.dot(first, flat[...], precision=HIGHEST, preferred_element_type=F32)
        flat[...] = left_one
        gram_two = contract(left_one, left_one, 1, 1, HIGHEST)

        remote(raw_slots.at[0:7], raw_slots.at[0:7], dp_send, dp_recv, sibling).wait_recv()
        raw[ranks(d)] = jnp.sum(raw_slots[...], axis=0)
        for k in (6, 2, 5, 7, 1, 3, 4):
            remote(raw.at[ranks(d)], raw.at[ranks(d)], dpg_send, dpg_recv, (dp_device(k), t)).start()

        second = inverse_cholesky(gram_two)

        @pl.when(step == ITERS - 1)
        def _():
            basis = jnp.dot(second, flat[...], precision=HIGHEST, preferred_element_type=F32)
            high, middle, _ = terms(basis)
            for i, term in enumerate((high, middle, high, middle)):
                basis_terms[i * R : (i + 1) * R] = term

        both_sweeps = jnp.dot(second, first, precision=HIGHEST, preferred_element_type=F32) * (1.0 / REPL)

        for j in range(CHUNKS):
            cross_copy(j).wait_send()
            fwd_copy(j).wait_send()
        remote(slots.at[0:63], slots.at[0:63], rs_send, rs_recv, sibling).wait_send()
        remote(left.at[0:63], left.at[0:63], ag_send, ag_recv.at[0], sibling).wait_send()
        remote(raw_slots.at[0:7], raw_slots.at[0:7], dp_send, dp_recv, sibling).wait_send()
        remote(raw_slots.at[0:7], raw_slots.at[0:7], dpg_send, dpg_recv, sibling).wait()

        right = jnp.dot(both_sweeps, raw[...], precision=HIGHEST, preferred_element_type=F32)
        right_out[...] = right
        set_right(right)
        return 0

    lax.fori_loop(0, ITERS, iteration, 0)

    high, middle, _ = terms(right_out[...])
    right_terms = jnp.concatenate([high, high, middle, middle], axis=0)

    def out_copy(b, slot):
        rows = pl.ds(pl.multiple_of(b * BLOCK, BLOCK), BLOCK)
        return pltpu.make_async_copy(stage.at[slot], error_out.at[0, rows], out_sem.at[slot])

    def finish(b, _):
        slot = lax.rem(b, 2)

        @pl.when(b >= 2)
        def _():
            out_copy(b - 2, slot).wait()

        rows = pl.ds(pl.multiple_of(b * BLOCK, BLOCK), BLOCK)
        approx = contract(basis_terms[:, rows], right_terms, 0, 0)
        block = both[rows, :]
        merged = block[:, 0:COLS].astype(F32) + block[:, COLS : 2 * COLS].astype(F32)
        stage[slot] = (merged - approx).astype(BF16)
        out_copy(b, slot).start()
        return 0

    count = D // BLOCK
    lax.fori_loop(0, count, finish, 0)
    out_copy(count - 2, count % 2).wait()
    out_copy(count - 1, (count - 1) % 2).wait()


def shards(gradient, error_in, warm_start):
    dma = pltpu.SemaphoreType.DMA
    return pl.pallas_call(
        kernel,
        name="power_iterations",
        out_shape=(
            jax.ShapeDtypeStruct((R, COLS), F32),
            jax.ShapeDtypeStruct((1, D, COLS), BF16),
        ),
        in_specs=[
            pl.BlockSpec(memory_space=pl.ANY),
            pl.BlockSpec(memory_space=pl.ANY),
            pl.BlockSpec(memory_space=pltpu.VMEM),
        ],
        out_specs=(pl.BlockSpec(memory_space=pltpu.VMEM), pl.BlockSpec(memory_space=pl.ANY)),
        scratch_shapes=[
            pltpu.VMEM((D, 2 * COLS), BF16),
            pltpu.VMEM((3 * R, 2 * COLS), BF16),
            pltpu.VMEM((128, PIECE, 128), F32),
            pltpu.VMEM((CHUNKS, 16, PIECE, 128), F32),
            pltpu.VMEM((CHUNKS, 16, PIECE, 128), F32),
            pltpu.VMEM((64, PIECE, 128), F32),
            pltpu.VMEM((128, PIECE, 128), F32),
            pltpu.VMEM((R, D), F32),
            pltpu.VMEM((R, COLS), F32),
            pltpu.VMEM((REPL, 8, COLS), F32),
            pltpu.VMEM((R, COLS), F32),
            pltpu.VMEM((4 * R, D), BF16),
            pltpu.VMEM((2, BLOCK, COLS), BF16),
            dma((CHUNKS, 2)),
            dma((CHUNKS,)),
            dma((CHUNKS,)),
            dma(()),
            dma(()),
            dma(()),
            dma((CHUNKS,)),
            dma((CHUNKS,)),
            dma((CHUNKS,)),
            dma(()),
            dma(()),
            dma(()),
            dma(()),
            dma((2,)),
        ],
        compiler_params=pltpu.CompilerParams(
            collective_id=0, has_side_effects=True, vmem_limit_bytes=56 * 1024 * 1024
        ),
    )(gradient, error_in, warm_start)


def solution(mesh):
    in_specs = (P("dp", None, "tensor"), P("dp", None, "tensor"), P(None, "tensor"))
    out_specs = (P(None, "tensor"), P("dp", None, "tensor"))
    return jax.shard_map(shards, mesh=mesh, in_specs=in_specs, out_specs=out_specs, check_vma=False)
```

```python
import jax
import jax.numpy as jnp
from jax import lax
from jax.experimental import pallas as pl
from jax.experimental.pallas import tpu as pltpu
from jax.sharding import PartitionSpec as P

ITERS = 4
REPL = 8
R = 64
D = 4096
COLS = 896
CHUNKS = 4
ROWS = D // CHUNKS
PIECE = 16
BLOCK = 512
VMEM_LIMIT = 58 * 1024 * 1024
MESH = pl.DeviceIdType.MESH
F32 = jnp.float32
BF16 = jnp.bfloat16
HIGHEST = lax.Precision.HIGHEST


def hops(step):
    return min(step, 4 - step)


OFFSETS = sorted(
    [(i, j, k) for i in range(4) for j in range(4) for k in range(4) if i + j + k],
    key=lambda o: -sum(map(hops, o)),
)


def terms(value):
    high = value.astype(BF16)
    rest = value - high.astype(F32)
    middle = rest.astype(BF16)
    low = (rest - middle.astype(F32)).astype(BF16)
    return high, middle, low


def sum_terms(product):
    return product[0:R] + product[R : 2 * R] + product[2 * R : 3 * R]


def contract(a, b, dim_a, dim_b, precision=None):
    return lax.dot_general(
        a, b, (((dim_a,), (dim_b,)), ((), ())), precision=precision, preferred_element_type=F32
    )


def inverse_cholesky(gram):
    ahead = 8
    lane = lax.broadcasted_iota(jnp.int32, (R, 2 * R), 1)
    sub = lax.broadcasted_iota(jnp.int32, (R, 2 * R), 0)
    work = jnp.concatenate([gram, jnp.zeros((R, R), F32)], axis=1)
    work = jnp.where(lane == sub + R, 1.0, work)
    for j in range(0, R, ahead):
        cols = [jnp.broadcast_to(work[:, j + k : j + k + 1], (R, 2 * R)) for k in range(ahead)]
        rows = [work[j + k : j + k + 1, :] for k in range(ahead)]
        factors = []
        for k in range(ahead):
            pivot = 1.0 / cols[k][j + k : j + k + 1, :]
            factor = jnp.where(sub > j + k, cols[k] * pivot, 0.0)
            factors.append(factor)
            for m in range(k + 1, ahead):
                cols[m] = cols[m] - factor * cols[m][j + k : j + k + 1, :]
                rows[m] = rows[m] - factor[j + m : j + m + 1, :] * rows[k]
        for k in range(ahead):
            work = work - factors[k] * rows[k]
    diagonal = jnp.sum(jnp.where(lane == sub, work, 0.0), axis=1, keepdims=True)
    return work[:, R:] * lax.rsqrt(diagonal)


def kernel(
    gradient, error, warm, basis_terms, right_out,
    both, turned, rr, part, cross, mine, slots, left, flat, raw_part, raw_slots, raw, sweeps,
    load_sem, cross_send, cross_recv, rs_send, rs_recv, ag_send, ag_recv, fwd_send, fwd_recv,
    dp_send, dp_recv, dpg_send, dpg_recv,
):
    d, t = lax.axis_index("dp"), lax.axis_index("tensor")
    x, y, z, c = d % 4, (t // 8) * 2 + d // 4, (t // 2) % 4, t % 2
    other = 1 - c
    group = (x + y + z) % 4
    place = x * 4 + y
    chip = place * 4 + z
    own = group * 32 + c * 16 + place

    def device(i, j, k):
        return ((j % 2) * 4 + i, (j // 2) * 8 + k * 2 + c)

    def away(o):
        return device((x + o[0]) % 4, (y + o[1]) % 4, (z + o[2]) % 4)

    sibling = (d, (t // 2) * 2 + other)

    def load(j):
        rows = pl.ds(j * ROWS, ROWS)
        return (
            pltpu.make_async_copy(gradient.at[0, rows], both.at[rows, 0:COLS], load_sem.at[j, 0]),
            pltpu.make_async_copy(error.at[0, rows], both.at[rows, COLS : 2 * COLS], load_sem.at[j, 1]),
        )

    for j in range(CHUNKS):
        for copy in load(j):
            copy.start()

    barrier = pltpu.get_barrier_semaphore()
    for o in OFFSETS:
        pl.semaphore_signal(barrier, 1, device_id=away(o), device_id_type=MESH)
    pl.semaphore_signal(barrier, 1, device_id=sibling, device_id_type=MESH)

    def set_right(value):
        for i, term in enumerate(terms(value)):
            rr[i * R : (i + 1) * R, 0:COLS] = term
            rr[i * R : (i + 1) * R, COLS : 2 * COLS] = term

    set_right(warm[...])

    def remote(src, dst, send, recv, target):
        return pltpu.make_async_remote_copy(src, dst, send, recv, device_id=target, device_id_type=MESH)

    def cross_copy(j):
        return remote(part.at[pl.ds(j * 32 + other * 16, 16)], cross.at[j], cross_send.at[j], cross_recv.at[j], sibling)

    def fwd_copy(j):
        half = left.at[pl.ds(j * 32 + c * 16, 16)]
        return remote(half, half, fwd_send.at[j], fwd_recv.at[j], sibling)

    def keep(j, product):
        product = sum_terms(product)
        for b in range(8):
            part[pl.ds(j * 32 + b * 4, 4)] = product[:, b * 128 : (b + 1) * 128].reshape(4, PIECE, 128)

    def row_chunk(j):
        return pl.ds(pl.multiple_of(j * ROWS, ROWS), ROWS)

    def loaded(j):
        rows = row_chunk(j)
        pltpu.make_async_copy(gradient.at[0, rows], both.at[rows, 0:COLS], load_sem.at[j, 0]).wait()
        pltpu.make_async_copy(error.at[0, rows], both.at[rows, COLS : 2 * COLS], load_sem.at[j, 1]).wait()

    def first_product(j):
        loaded(j)
        keep(j, contract(rr[...], both[row_chunk(j), :], 1, 1))

    def scatter_chunk(j):
        cross_copy(j).wait_recv()
        mine[j] = part[pl.ds(j * 32 + c * 16, 16)] + cross[j]
        for r in (10, 2, 8, 6, 14, 9, 11, 5, 7, 13, 15, 1, 3, 4, 12, 0):
            i, k = (x + r // 4) % 4, (y + r % 4) % 4
            copy = remote(mine.at[j, i * 4 + k], slots.at[chip], rs_send, rs_recv, device(i, k, (j - i - k + 8) % 4))
            if r:
                copy.start()
            else:

                @pl.when(j != group)
                def _():
                    copy.start()

                @pl.when(j == group)
                def _():
                    slots[chip] = mine[j, place]

    def gathered(j):
        @pl.when(j == group)
        def _():
            remote(left.at[0:15], left.at[0:15], ag_send, ag_recv.at[j], sibling).wait_recv()

        @pl.when(j != group)
        def _():
            remote(left.at[0:16], left.at[0:16], ag_send, ag_recv.at[j], sibling).wait_recv()

        fwd_copy(j).start()

    def right_chunk(j, carry):
        @pl.when(j < CHUNKS - 1)
        def _():
            gathered(j + 1)

        fwd_copy(j).wait_recv()
        rows = pl.ds(pl.multiple_of(j * ROWS, ROWS), ROWS)
        blocks = left[pl.ds(j * 32, 32)].reshape(8, R, 128)
        value = jnp.concatenate([blocks[b] for b in range(8)], axis=1)
        flat[:, rows] = value
        stacked = jnp.concatenate(terms(value), axis=0)
        product = sum_terms(contract(stacked, both[rows, :], 1, 0))
        raw_part[...] += product[:, 0:COLS] + product[:, COLS : 2 * COLS]
        return carry

    def ranks(owner):
        return pl.ds(pl.multiple_of(owner * 8, 8), 8)

    first_product(0)
    pl.semaphore_wait(barrier, len(OFFSETS) + 1)

    def iteration(step, _):
        def left_step(j, carry):
            @pl.when((step == 0) & (j > 0))
            def _():
                first_product(j)

            @pl.when(step > 0)
            def _():
                keep(j, jnp.dot(rr[...], turned[:, row_chunk(j)], preferred_element_type=F32))

            cross_copy(j).start()

            @pl.when(j > 0)
            def _():
                scatter_chunk(j - 1)

            return carry

        lax.fori_loop(0, CHUNKS, left_step, 0)
        scatter_chunk(CHUNKS - 1)

        @pl.when(step == 0)
        def _():
            def turn(j, carry):
                rows = pl.ds(pl.multiple_of(j * BLOCK, BLOCK), BLOCK)
                turned[:, rows] = both[rows, :].T
                return carry

            lax.fori_loop(0, D // BLOCK, turn, 0)

        raw_part[...] = jnp.zeros_like(raw_part)
        remote(slots.at[0:63], slots.at[0:63], rs_send, rs_recv, sibling).wait_recv()
        left[own] = jnp.sum(slots[...], axis=0)
        for o in OFFSETS:
            remote(left.at[own], left.at[own], ag_send, ag_recv.at[group], away(o)).start()

        gathered(0)
        lax.fori_loop(0, CHUNKS, right_chunk, 0)

        def dp_device(k):
            return lax.rem(d + k, REPL)

        for k in (6, 2, 5, 7, 1, 3, 4):
            owner = dp_device(k)
            remote(raw_part.at[ranks(owner)], raw_slots.at[d], dp_send, dp_recv, (owner, t)).start()
        raw_slots[d] = raw_part[ranks(d)]

        @pl.when(step < ITERS)
        def _():
            sweeps[0] = inverse_cholesky(contract(flat[...], flat[...], 1, 1, HIGHEST))

        remote(raw_slots.at[0:7], raw_slots.at[0:7], dp_send, dp_recv, sibling).wait_recv()
        raw[ranks(d)] = jnp.sum(raw_slots[...], axis=0)
        for k in (6, 2, 5, 7, 1, 3, 4):
            remote(raw.at[ranks(d)], raw.at[ranks(d)], dpg_send, dpg_recv, (dp_device(k), t)).start()

        @pl.when(step < ITERS)
        def _():
            first = sweeps[0]
            left_one = jnp.dot(first, flat[...], precision=HIGHEST, preferred_element_type=F32)
            flat[...] = left_one
            second = inverse_cholesky(contract(left_one, left_one, 1, 1, HIGHEST))
            sweeps[1] = second
            sweeps[0] = jnp.dot(second, first, precision=HIGHEST, preferred_element_type=F32) * (1.0 / REPL)

        @pl.when(step == ITERS - 1)
        def _():
            basis = jnp.dot(sweeps[1], flat[...], precision=HIGHEST, preferred_element_type=F32)
            high, middle, _ = terms(basis)
            basis_terms[...] = jnp.concatenate([high, middle, high, middle], axis=0).T

        for j in range(CHUNKS):
            cross_copy(j).wait_send()
            fwd_copy(j).wait_send()
        remote(slots.at[0:63], slots.at[0:63], rs_send, rs_recv, sibling).wait_send()
        remote(left.at[0:63], left.at[0:63], ag_send, ag_recv.at[0], sibling).wait_send()
        remote(raw_slots.at[0:7], raw_slots.at[0:7], dp_send, dp_recv, sibling).wait_send()
        remote(raw_slots.at[0:7], raw_slots.at[0:7], dpg_send, dpg_recv, sibling).wait()

        right = jnp.dot(sweeps[0], raw[...], precision=HIGHEST, preferred_element_type=F32)
        right_out[...] = right
        set_right(right)
        return 0

    lax.fori_loop(0, ITERS, iteration, 0)


def finish(gradient, error, basis_terms, right, right_out, error_out):
    @pl.when(pl.program_id(0) == 0)
    def _():
        right_out[...] = right[...]

    high, middle, _ = terms(right[...])
    right_terms = jnp.concatenate([high, high, middle, middle], axis=0)
    approx = jnp.dot(basis_terms[...], right_terms, preferred_element_type=F32)
    merged = gradient[0].astype(F32) + error[0].astype(F32)
    error_out[0] = (merged - approx).astype(BF16)


def shards(gradient, error_in, warm_start):
    dma = pltpu.SemaphoreType.DMA
    block = pl.BlockSpec((1, BLOCK, COLS), lambda i: (0, i, 0))
    whole = pl.BlockSpec(memory_space=pltpu.VMEM)
    basis_terms, right = pl.pallas_call(
        kernel,
        name="power_iterations",
        out_shape=(
            jax.ShapeDtypeStruct((D, 4 * R), BF16),
            jax.ShapeDtypeStruct((R, COLS), F32),
        ),
        in_specs=[
            pl.BlockSpec(memory_space=pltpu.HBM),
            pl.BlockSpec(memory_space=pltpu.HBM),
            whole,
        ],
        out_specs=(whole, whole),
        scratch_shapes=[
            pltpu.VMEM((D, 2 * COLS), BF16),
            pltpu.VMEM((2 * COLS, D), BF16),
            pltpu.VMEM((3 * R, 2 * COLS), BF16),
            pltpu.VMEM((128, PIECE, 128), F32),
            pltpu.VMEM((CHUNKS, 16, PIECE, 128), F32),
            pltpu.VMEM((CHUNKS, 16, PIECE, 128), F32),
            pltpu.VMEM((64, PIECE, 128), F32),
            pltpu.VMEM((128, PIECE, 128), F32),
            pltpu.VMEM((R, D), F32),
            pltpu.VMEM((R, COLS), F32),
            pltpu.VMEM((REPL, 8, COLS), F32),
            pltpu.VMEM((R, COLS), F32),
            pltpu.VMEM((2, R, R), F32),
            dma((CHUNKS, 2)),
            dma((CHUNKS,)),
            dma((CHUNKS,)),
            dma(()),
            dma(()),
            dma(()),
            dma((CHUNKS,)),
            dma((CHUNKS,)),
            dma((CHUNKS,)),
            dma(()),
            dma(()),
            dma(()),
            dma(()),
        ],
        compiler_params=pltpu.CompilerParams(
            collective_id=0, has_side_effects=True, vmem_limit_bytes=VMEM_LIMIT
        ),
    )(gradient, error_in, warm_start)
    return pl.pallas_call(
        finish,
        name="error_feedback",
        grid=(D // BLOCK,),
        out_shape=(
            jax.ShapeDtypeStruct((R, COLS), F32),
            jax.ShapeDtypeStruct((1, D, COLS), BF16),
        ),
        in_specs=[block, block, pl.BlockSpec((BLOCK, 4 * R), lambda i: (i, 0)), whole],
        out_specs=(whole, block),
        compiler_params=pltpu.CompilerParams(vmem_limit_bytes=VMEM_LIMIT),
    )(gradient, error_in, basis_terms, right)


def solution(mesh):
    in_specs = (P("dp", None, "tensor"), P("dp", None, "tensor"), P(None, "tensor"))
    out_specs = (P(None, "tensor"), P("dp", None, "tensor"))
    return jax.shard_map(shards, mesh=mesh, in_specs=in_specs, out_specs=out_specs, check_vma=False)
```

```python
import jax
import jax.numpy as jnp
from jax import lax
from jax.experimental import pallas as pl
from jax.experimental.pallas import tpu as pltpu
from jax.sharding import PartitionSpec as P

ITERS = 4
REPL = 8
R = 64
D = 4096
COLS = 896
CHUNKS = 4
ROWS = D // CHUNKS
PIECE = 16
BLOCK = 512
VMEM_LIMIT = 46 * 1024 * 1024
MESH = pl.DeviceIdType.MESH
F32 = jnp.float32
BF16 = jnp.bfloat16
HIGHEST = lax.Precision.HIGHEST


def hops(step):
    return min(step, 4 - step)


OFFSETS = sorted(
    [(i, j, k) for i in range(4) for j in range(4) for k in range(4) if i + j + k],
    key=lambda o: -sum(map(hops, o)),
)

DP_OFFSETS = ((1, 2), (1, 1), (1, 3), (0, 2), (0, 1), (0, 3), (1, 0))


def terms(value):
    high = value.astype(BF16)
    rest = value - high.astype(F32)
    middle = rest.astype(BF16)
    low = (rest - middle.astype(F32)).astype(BF16)
    return high, middle, low


def sum_terms(product):
    return product[0:R] + product[R : 2 * R] + product[2 * R : 3 * R]


def contract(a, b, dim_a, dim_b, precision=None):
    return lax.dot_general(
        a, b, (((dim_a,), (dim_b,)), ((), ())), precision=precision, preferred_element_type=F32
    )


def inverse_cholesky(gram):
    ahead = 8
    lane = lax.broadcasted_iota(jnp.int32, (R, 2 * R), 1)
    sub = lax.broadcasted_iota(jnp.int32, (R, 2 * R), 0)
    work = jnp.concatenate([gram, jnp.zeros((R, R), F32)], axis=1)
    work = jnp.where(lane == sub + R, 1.0, work)
    for j in range(0, R, ahead):
        cols = [jnp.broadcast_to(work[:, j + k : j + k + 1], (R, 2 * R)) for k in range(ahead)]
        rows = [work[j + k : j + k + 1, :] for k in range(ahead)]
        factors = []
        for k in range(ahead):
            pivot = 1.0 / cols[k][j + k : j + k + 1, :]
            factor = jnp.where(sub > j + k, cols[k] * pivot, 0.0)
            factors.append(factor)
            for m in range(k + 1, ahead):
                cols[m] = cols[m] - factor * cols[m][j + k : j + k + 1, :]
                rows[m] = rows[m] - factor[j + m : j + m + 1, :] * rows[k]
        for k in range(ahead):
            work = work - factors[k] * rows[k]
    diagonal = jnp.sum(jnp.where(lane == sub, work, 0.0), axis=1, keepdims=True)
    return work[:, R:] * lax.rsqrt(diagonal)


def kernel(
    gradient, error, warm, basis_terms, right_out,
    both, turned, rr, part, cross, mine, slots, left, flat, raw_part, raw_slots, raw, sweeps,
    load_sem, cross_send, cross_recv, rs_send, rs_recv, ag_send, ag_recv, fwd_send, fwd_recv,
    dp_send, dp_recv, dpg_send, dpg_recv,
):
    d, t = lax.axis_index("dp"), lax.axis_index("tensor")
    x, y, z, c = d % 4, (t // 8) * 2 + d // 4, (t // 2) % 4, t % 2
    other = 1 - c
    group = (x + y + z) % 4
    place = x * 4 + y
    chip = place * 4 + z
    own = group * 32 + c * 16 + place

    def device(i, j, k):
        return ((j % 2) * 4 + i, (j // 2) * 8 + k * 2 + c)

    def away(o):
        return device((x + o[0]) % 4, (y + o[1]) % 4, (z + o[2]) % 4)

    sibling = (d, (t // 2) * 2 + other)

    def load(j):
        rows = pl.ds(j * ROWS, ROWS)
        return (
            pltpu.make_async_copy(gradient.at[0, rows], both.at[rows, 0:COLS], load_sem.at[j, 0]),
            pltpu.make_async_copy(error.at[0, rows], both.at[rows, COLS : 2 * COLS], load_sem.at[j, 1]),
        )

    for j in range(CHUNKS):
        for copy in load(j):
            copy.start()

    barrier = pltpu.get_barrier_semaphore()
    for o in OFFSETS:
        pl.semaphore_signal(barrier, 1, device_id=away(o), device_id_type=MESH)
    pl.semaphore_signal(barrier, 1, device_id=sibling, device_id_type=MESH)

    def set_right(value):
        for i, term in enumerate(terms(value)):
            rr[i * R : (i + 1) * R, 0:COLS] = term
            rr[i * R : (i + 1) * R, COLS : 2 * COLS] = term

    set_right(warm[...])

    def remote(src, dst, send, recv, target):
        return pltpu.make_async_remote_copy(src, dst, send, recv, device_id=target, device_id_type=MESH)

    def cross_copy(j):
        return remote(part.at[pl.ds(j * 32 + other * 16, 16)], cross.at[j], cross_send.at[j], cross_recv.at[j], sibling)

    def fwd_copy(j):
        half = left.at[pl.ds(j * 32 + c * 16, 16)]
        return remote(half, half, fwd_send.at[j], fwd_recv.at[j], sibling)

    def keep(j, product):
        product = sum_terms(product)
        for b in range(8):
            part[pl.ds(j * 32 + b * 4, 4)] = product[:, b * 128 : (b + 1) * 128].reshape(4, PIECE, 128)

    def row_chunk(j):
        return pl.ds(pl.multiple_of(j * ROWS, ROWS), ROWS)

    def loaded(j):
        rows = row_chunk(j)
        pltpu.make_async_copy(gradient.at[0, rows], both.at[rows, 0:COLS], load_sem.at[j, 0]).wait()
        pltpu.make_async_copy(error.at[0, rows], both.at[rows, COLS : 2 * COLS], load_sem.at[j, 1]).wait()

    def first_product(j):
        loaded(j)
        keep(j, contract(rr[...], both[row_chunk(j), :], 1, 1))

    def scatter_chunk(j):
        cross_copy(j).wait_recv()
        mine[j] = part[pl.ds(j * 32 + c * 16, 16)] + cross[j]
        for r in (10, 2, 8, 6, 14, 9, 11, 5, 7, 13, 15, 1, 3, 4, 12, 0):
            i, k = (x + r // 4) % 4, (y + r % 4) % 4
            copy = remote(mine.at[j, i * 4 + k], slots.at[chip], rs_send, rs_recv, device(i, k, (j - i - k + 8) % 4))
            if r:
                copy.start()
            else:

                @pl.when(j != group)
                def _():
                    copy.start()

                @pl.when(j == group)
                def _():
                    slots[chip] = mine[j, place]

    def gathered(j):
        @pl.when(j == group)
        def _():
            remote(left.at[0:15], left.at[0:15], ag_send, ag_recv.at[j], sibling).wait_recv()

        @pl.when(j != group)
        def _():
            remote(left.at[0:16], left.at[0:16], ag_send, ag_recv.at[j], sibling).wait_recv()

        fwd_copy(j).start()

    def right_chunk(j, carry):
        @pl.when(j < CHUNKS - 1)
        def _():
            gathered(j + 1)

        fwd_copy(j).wait_recv()
        rows = pl.ds(pl.multiple_of(j * ROWS, ROWS), ROWS)
        blocks = left[pl.ds(j * 32, 32)].reshape(8, R, 128)
        value = jnp.concatenate([blocks[b] for b in range(8)], axis=1)
        flat[:, rows] = value
        stacked = jnp.concatenate(terms(value), axis=0)
        product = sum_terms(contract(stacked, both[rows, :], 1, 0))
        raw_part[...] += product[:, 0:COLS] + product[:, COLS : 2 * COLS]
        return carry

    def dp_device(o):
        return ((d // 4 + o[0]) % 2) * 4 + (x + o[1]) % 4

    def ranks(owner):
        return pl.ds(pl.multiple_of(owner * 8, 8), 8)

    first_product(0)
    pl.semaphore_wait(barrier, len(OFFSETS) + 1)

    def iteration(step, _):
        def left_step(j, carry):
            @pl.when((step == 0) & (j > 0))
            def _():
                first_product(j)

            @pl.when(step > 0)
            def _():
                keep(j, jnp.dot(rr[...], turned[:, row_chunk(j)], preferred_element_type=F32))

            cross_copy(j).start()

            return carry

        lax.fori_loop(0, CHUNKS, left_step, 0)
        scatter_chunk(CHUNKS - 4)
        scatter_chunk(CHUNKS - 3)
        scatter_chunk(CHUNKS - 2)
        scatter_chunk(CHUNKS - 1)

        @pl.when(step == 0)
        def _():
            def turn(j, carry):
                rows = pl.ds(pl.multiple_of(j * BLOCK, BLOCK), BLOCK)
                turned[:, rows] = both[rows, :].T
                return carry

            lax.fori_loop(0, D // BLOCK, turn, 0)

        raw_part[...] = jnp.zeros_like(raw_part)
        remote(slots.at[0:63], slots.at[0:63], rs_send, rs_recv, sibling).wait_recv()
        left[own] = jnp.sum(slots[...], axis=0)
        for o in OFFSETS:
            remote(left.at[own], left.at[own], ag_send, ag_recv.at[group], away(o)).start()

        gathered(0)
        lax.fori_loop(0, CHUNKS, right_chunk, 0)

        for k in DP_OFFSETS:
            owner = dp_device(k)
            remote(raw_part.at[ranks(owner)], raw_slots.at[d], dp_send, dp_recv, (owner, t)).start()
        raw_slots[d] = raw_part[ranks(d)]

        @pl.when(step < ITERS)
        def _():
            sweeps[0] = inverse_cholesky(contract(flat[...], flat[...], 1, 1, HIGHEST))

        remote(raw_slots.at[0:7], raw_slots.at[0:7], dp_send, dp_recv, sibling).wait_recv()
        raw[ranks(d)] = jnp.sum(raw_slots[...], axis=0)
        for k in DP_OFFSETS:
            remote(raw.at[ranks(d)], raw.at[ranks(d)], dpg_send, dpg_recv, (dp_device(k), t)).start()

        @pl.when(step < ITERS)
        def _():
            first = sweeps[0]
            left_one = jnp.dot(first, flat[...], precision=HIGHEST, preferred_element_type=F32)
            flat[...] = left_one
            second = inverse_cholesky(contract(left_one, left_one, 1, 1, HIGHEST))
            sweeps[1] = second
            sweeps[0] = jnp.dot(second, first, precision=HIGHEST, preferred_element_type=F32) * (1.0 / REPL)

        @pl.when(step == ITERS - 1)
        def _():
            basis = jnp.dot(sweeps[1], flat[...], precision=HIGHEST, preferred_element_type=F32)
            high, middle, _ = terms(basis)
            basis_terms[...] = jnp.concatenate([high, middle, high, middle], axis=0).T

        for j in range(CHUNKS):
            cross_copy(j).wait_send()
            fwd_copy(j).wait_send()
        remote(slots.at[0:63], slots.at[0:63], rs_send, rs_recv, sibling).wait_send()
        remote(left.at[0:63], left.at[0:63], ag_send, ag_recv.at[0], sibling).wait_send()
        remote(raw_slots.at[0:7], raw_slots.at[0:7], dp_send, dp_recv, sibling).wait_send()
        remote(raw_slots.at[0:7], raw_slots.at[0:7], dpg_send, dpg_recv, sibling).wait()

        right = jnp.dot(sweeps[0], raw[...], precision=HIGHEST, preferred_element_type=F32)
        right_out[...] = right
        set_right(right)
        return 0

    lax.fori_loop(0, ITERS, iteration, 0)


def finish(gradient, error, basis_terms, right, right_out, error_out):
    @pl.when(pl.program_id(0) == 0)
    def _():
        right_out[...] = right[...]

    high, middle, _ = terms(right[...])
    right_terms = jnp.concatenate([high, high, middle, middle], axis=0)
    approx = jnp.dot(basis_terms[...], right_terms, preferred_element_type=F32)
    merged = gradient[0].astype(F32) + error[0].astype(F32)
    error_out[0] = (merged - approx).astype(BF16)


def shards(gradient, error_in, warm_start):
    dma = pltpu.SemaphoreType.DMA
    block = pl.BlockSpec((1, 1024, COLS), lambda i: (0, i, 0))
    whole = pl.BlockSpec(memory_space=pltpu.VMEM)
    basis_terms, right = pl.pallas_call(
        kernel,
        name="power_iterations",
        out_shape=(
            jax.ShapeDtypeStruct((D, 4 * R), BF16),
            jax.ShapeDtypeStruct((R, COLS), F32),
        ),
        in_specs=[
            pl.BlockSpec(memory_space=pltpu.HBM),
            pl.BlockSpec(memory_space=pltpu.HBM),
            whole,
        ],
        out_specs=(whole, whole),
        scratch_shapes=[
            pltpu.VMEM((D, 2 * COLS), BF16),
            pltpu.VMEM((2 * COLS, D), BF16),
            pltpu.VMEM((3 * R, 2 * COLS), BF16),
            pltpu.VMEM((128, PIECE, 128), F32),
            pltpu.VMEM((CHUNKS, 16, PIECE, 128), F32),
            pltpu.VMEM((CHUNKS, 16, PIECE, 128), F32),
            pltpu.VMEM((64, PIECE, 128), F32),
            pltpu.VMEM((128, PIECE, 128), F32),
            pltpu.VMEM((R, D), F32),
            pltpu.VMEM((R, COLS), F32),
            pltpu.VMEM((REPL, 8, COLS), F32),
            pltpu.VMEM((R, COLS), F32),
            pltpu.VMEM((2, R, R), F32),
            dma((CHUNKS, 2)),
            dma((CHUNKS,)),
            dma((CHUNKS,)),
            dma(()),
            dma(()),
            dma(()),
            dma((CHUNKS,)),
            dma((CHUNKS,)),
            dma((CHUNKS,)),
            dma(()),
            dma(()),
            dma(()),
            dma(()),
        ],
        compiler_params=pltpu.CompilerParams(
            collective_id=0, has_side_effects=True, vmem_limit_bytes=VMEM_LIMIT
        ),
    )(gradient, error_in, warm_start)
    return pl.pallas_call(
        finish,
        name="error_feedback",
        grid=(D // 1024,),
        out_shape=(
            jax.ShapeDtypeStruct((R, COLS), F32),
            jax.ShapeDtypeStruct((1, D, COLS), BF16),
        ),
        in_specs=[block, block, pl.BlockSpec((1024, 4 * R), lambda i: (i, 0)), whole],
        out_specs=(whole, block),
        compiler_params=pltpu.CompilerParams(vmem_limit_bytes=VMEM_LIMIT),
    )(gradient, error_in, basis_terms, right)


def solution(mesh):
    in_specs = (P("dp", None, "tensor"), P("dp", None, "tensor"), P(None, "tensor"))
    out_specs = (P(None, "tensor"), P("dp", None, "tensor"))
    return jax.shard_map(shards, mesh=mesh, in_specs=in_specs, out_specs=out_specs, check_vma=False)
```

```python
import jax
import jax.numpy as jnp
from jax import lax
from jax.experimental import pallas as pl
from jax.experimental.pallas import tpu as pltpu
from jax.sharding import PartitionSpec as P

ITERS = 4
REPL = 8
R = 64
D = 4096
COLS = 896
CHUNKS = 4
ROWS = D // CHUNKS
PIECE = 16
BLOCK = 1024
VMEM_LIMIT = 46 * 1024 * 1024
MESH = pl.DeviceIdType.MESH
F32 = jnp.float32
BF16 = jnp.bfloat16
HIGHEST = lax.Precision.HIGHEST


def hops(step):
    return min(step, 4 - step)


OFFSETS = sorted(
    [(i, j, k) for i in range(4) for j in range(4) for k in range(4) if i + j + k],
    key=lambda o: -sum(map(hops, o)),
)

DP_OFFSETS = ((1, 2), (1, 1), (1, 3), (0, 2), (0, 1), (0, 3), (1, 0))


def terms(value):
    high = value.astype(BF16)
    rest = value - high.astype(F32)
    middle = rest.astype(BF16)
    low = (rest - middle.astype(F32)).astype(BF16)
    return high, middle, low


def sum_terms(product):
    return product[0:R] + product[R : 2 * R] + product[2 * R : 3 * R]


def contract(a, b, dim_a, dim_b, precision=None):
    return lax.dot_general(
        a, b, (((dim_a,), (dim_b,)), ((), ())), precision=precision, preferred_element_type=F32
    )


def inverse_cholesky(gram):
    ahead = 8
    lane = lax.broadcasted_iota(jnp.int32, (R, 2 * R), 1)
    sub = lax.broadcasted_iota(jnp.int32, (R, 2 * R), 0)
    work = jnp.concatenate([gram, jnp.zeros((R, R), F32)], axis=1)
    work = jnp.where(lane == sub + R, 1.0, work)
    for j in range(0, R, ahead):
        cols = [jnp.broadcast_to(work[:, j + k : j + k + 1], (R, 2 * R)) for k in range(ahead)]
        rows = [work[j + k : j + k + 1, :] for k in range(ahead)]
        factors = []
        for k in range(ahead):
            pivot = 1.0 / cols[k][j + k : j + k + 1, :]
            factor = jnp.where(sub > j + k, cols[k] * pivot, 0.0)
            factors.append(factor)
            for m in range(k + 1, ahead):
                cols[m] = cols[m] - factor * cols[m][j + k : j + k + 1, :]
                rows[m] = rows[m] - factor[j + m : j + m + 1, :] * rows[k]
        for k in range(ahead):
            work = work - factors[k] * rows[k]
    diagonal = jnp.sum(jnp.where(lane == sub, work, 0.0), axis=1, keepdims=True)
    return work[:, R:] * lax.rsqrt(diagonal)


def kernel(
    gradient, error, warm, flat, second_out, right_out,
    both, turned, rr, part, cross, mine, slots, left, raw_part, raw_slots, raw, first_sweep,
    load_sem, cross_send, cross_recv, rs_send, rs_recv, ag_send, ag_recv, fwd_send, fwd_recv,
    dp_send, dp_recv, dpg_send, dpg_recv,
):
    d, t = lax.axis_index("dp"), lax.axis_index("tensor")
    x, y, z, c = d % 4, (t // 8) * 2 + d // 4, (t // 2) % 4, t % 2
    other = 1 - c
    group = (x + y + z) % 4
    place = x * 4 + y
    chip = place * 4 + z
    own = group * 32 + c * 16 + place

    xs = [(x + i) % 4 for i in range(4)]
    ys = [(y + i) % 4 for i in range(4)]
    dp_of_y = [(j % 2) * 4 for j in ys]
    tensor_of_y = [(j // 2) * 8 for j in ys]
    tensor_of_z = [((z + i) % 4) * 2 + c for i in range(4)]
    xs_places = [i * 4 for i in xs]
    dp_of_step = [((d // 4 + i) % 2) * 4 for i in range(2)]

    def away(o):
        return (dp_of_y[o[1]] + xs[o[0]], tensor_of_y[o[1]] + tensor_of_z[o[2]])

    sibling = (d, (t // 2) * 2 + other)

    def load(j):
        rows = pl.ds(j * ROWS, ROWS)
        return (
            pltpu.make_async_copy(gradient.at[0, rows], both.at[rows, 0:COLS], load_sem.at[j, 0]),
            pltpu.make_async_copy(error.at[0, rows], both.at[rows, COLS : 2 * COLS], load_sem.at[j, 1]),
        )

    for j in range(CHUNKS):
        for copy in load(j):
            copy.start()

    barrier = pltpu.get_barrier_semaphore()
    for o in OFFSETS:
        pl.semaphore_signal(barrier, 1, device_id=away(o), device_id_type=MESH)
    pl.semaphore_signal(barrier, 1, device_id=sibling, device_id_type=MESH)

    def set_right(value):
        for i, term in enumerate(terms(value)):
            rr[i * R : (i + 1) * R, 0:COLS] = term
            rr[i * R : (i + 1) * R, COLS : 2 * COLS] = term

    set_right(warm[...])

    def remote(src, dst, send, recv, target):
        return pltpu.make_async_remote_copy(src, dst, send, recv, device_id=target, device_id_type=MESH)

    def cross_copy(j):
        return remote(part.at[pl.ds(j * 32 + other * 16, 16)], cross.at[j], cross_send.at[j], cross_recv.at[j], sibling)

    def fwd_copy(j):
        half = left.at[pl.ds(j * 32 + c * 16, 16)]
        return remote(half, half, fwd_send.at[j], fwd_recv.at[j], sibling)

    def keep(j, product):
        product = sum_terms(product)
        for b in range(8):
            part[pl.ds(j * 32 + b * 4, 4)] = product[:, b * 128 : (b + 1) * 128].reshape(4, PIECE, 128)

    def row_chunk(j):
        return pl.ds(pl.multiple_of(j * ROWS, ROWS), ROWS)

    def loaded(j):
        rows = row_chunk(j)
        pltpu.make_async_copy(gradient.at[0, rows], both.at[rows, 0:COLS], load_sem.at[j, 0]).wait()
        pltpu.make_async_copy(error.at[0, rows], both.at[rows, COLS : 2 * COLS], load_sem.at[j, 1]).wait()

    def first_product(j):
        loaded(j)
        keep(j, contract(rr[...], both[row_chunk(j), :], 1, 1))

    def scatter_chunk(j):
        cross_copy(j).wait_recv()
        mine[j] = part[pl.ds(j * 32 + c * 16, 16)] + cross[j]
        def send_from(g):
            @pl.when(group == g)
            def _():
                for o in OFFSETS:
                    if (sum(o) + g - j) % 4 == 0:
                        source = mine.at[j, xs_places[o[0]] + ys[o[1]]]
                        remote(source, slots.at[chip], rs_send, rs_recv, away(o)).start()
                if g == j:
                    slots[chip] = mine[j, place]

        for g in range(4):
            send_from(g)

    def gathered(j):
        @pl.when(j == group)
        def _():
            remote(left.at[0:15], left.at[0:15], ag_send, ag_recv.at[j], sibling).wait_recv()

        @pl.when(j != group)
        def _():
            remote(left.at[0:16], left.at[0:16], ag_send, ag_recv.at[j], sibling).wait_recv()

        fwd_copy(j).start()

    def right_chunk(j, carry):
        @pl.when(j < CHUNKS - 1)
        def _():
            gathered(j + 1)

        fwd_copy(j).wait_recv()
        rows = pl.ds(pl.multiple_of(j * ROWS, ROWS), ROWS)
        blocks = left[pl.ds(j * 32, 32)].reshape(8, R, 128)
        value = jnp.concatenate([blocks[b] for b in range(8)], axis=1)
        flat[:, rows] = value
        stacked = jnp.concatenate(terms(value), axis=0)
        product = sum_terms(contract(stacked, both[rows, :], 1, 0))
        raw_part[...] += product[:, 0:COLS] + product[:, COLS : 2 * COLS]
        return carry

    def dp_device(o):
        return dp_of_step[o[0]] + xs[o[1]]

    def ranks(owner):
        return pl.ds(pl.multiple_of(owner * 8, 8), 8)

    first_product(0)
    pl.semaphore_wait(barrier, len(OFFSETS) + 1)

    def iteration(step, _):
        def left_step(j, carry):
            @pl.when((step == 0) & (j > 0))
            def _():
                first_product(j)

            @pl.when(step > 0)
            def _():
                keep(j, jnp.dot(rr[...], turned[:, row_chunk(j)], preferred_element_type=F32))

            cross_copy(j).start()
            return carry

        lax.fori_loop(0, CHUNKS, left_step, 0)
        scatter_chunk(CHUNKS - 4)
        scatter_chunk(CHUNKS - 3)
        scatter_chunk(CHUNKS - 2)
        scatter_chunk(CHUNKS - 1)

        @pl.when(step == 0)
        def _():
            def turn(j, carry):
                rows = row_chunk(j)
                turned[:, rows] = both[rows, :].T
                return carry

            lax.fori_loop(0, CHUNKS, turn, 0)

        raw_part[...] = jnp.zeros_like(raw_part)
        remote(slots.at[0:63], slots.at[0:63], rs_send, rs_recv, sibling).wait_recv()
        left[own] = jnp.sum(slots[...], axis=0)
        for o in OFFSETS:
            remote(left.at[own], left.at[own], ag_send, ag_recv.at[group], away(o)).start()

        gathered(0)
        lax.fori_loop(0, CHUNKS, right_chunk, 0)

        for k in DP_OFFSETS:
            owner = dp_device(k)
            remote(raw_part.at[ranks(owner)], raw_slots.at[d], dp_send, dp_recv, (owner, t)).start()
        raw_slots[d] = raw_part[ranks(d)]

        @pl.when(step < ITERS)
        def _():
            first_sweep[...] = inverse_cholesky(contract(flat[...], flat[...], 1, 1, HIGHEST))

        remote(raw_slots.at[0:7], raw_slots.at[0:7], dp_send, dp_recv, sibling).wait_recv()
        raw[ranks(d)] = jnp.sum(raw_slots[...], axis=0)
        for k in DP_OFFSETS:
            remote(raw.at[ranks(d)], raw.at[ranks(d)], dpg_send, dpg_recv, (dp_device(k), t)).start()

        @pl.when(step < ITERS)
        def _():
            first = first_sweep[...]
            left_one = jnp.dot(first, flat[...], precision=HIGHEST, preferred_element_type=F32)
            flat[...] = left_one
            second = inverse_cholesky(contract(left_one, left_one, 1, 1, HIGHEST))
            second_out[...] = second
            first_sweep[...] = jnp.dot(second, first, precision=HIGHEST, preferred_element_type=F32) * (1.0 / REPL)

        for j in range(CHUNKS):
            cross_copy(j).wait_send()
            fwd_copy(j).wait_send()
        remote(slots.at[0:63], slots.at[0:63], rs_send, rs_recv, sibling).wait_send()
        remote(left.at[0:63], left.at[0:63], ag_send, ag_recv.at[0], sibling).wait_send()
        remote(raw_slots.at[0:7], raw_slots.at[0:7], dp_send, dp_recv, sibling).wait_send()
        remote(raw_slots.at[0:7], raw_slots.at[0:7], dpg_send, dpg_recv, sibling).wait()

        right = jnp.dot(first_sweep[...], raw[...], precision=HIGHEST, preferred_element_type=F32)
        right_out[...] = right
        set_right(right)
        return 0

    lax.fori_loop(0, ITERS, iteration, 0)


def finish(gradient, error, left_one, second, right, right_out, error_out):
    @pl.when(pl.program_id(0) == 0)
    def _():
        right_out[...] = right[...]

    high, middle, _ = terms(right[...])
    right_terms = jnp.concatenate([high, high, middle, middle], axis=0)
    rows = pl.ds(pl.multiple_of(pl.program_id(0) * BLOCK, BLOCK), BLOCK)
    basis = jnp.dot(second[...], left_one[:, rows], precision=HIGHEST, preferred_element_type=F32)
    basis_high, basis_middle, _ = terms(basis)
    basis_terms = jnp.concatenate([basis_high, basis_middle, basis_high, basis_middle], axis=0).T
    approx = jnp.dot(basis_terms, right_terms, preferred_element_type=F32)
    merged = gradient[0].astype(F32) + error[0].astype(F32)
    error_out[0] = (merged - approx).astype(BF16)


def shards(gradient, error_in, warm_start):
    dma = pltpu.SemaphoreType.DMA
    block = pl.BlockSpec((1, BLOCK, COLS), lambda i: (0, i, 0))
    whole = pl.BlockSpec(memory_space=pltpu.VMEM)
    left_one, second, right = pl.pallas_call(
        kernel,
        name="power_iterations",
        out_shape=(
            jax.ShapeDtypeStruct((R, D), F32),
            jax.ShapeDtypeStruct((R, R), F32),
            jax.ShapeDtypeStruct((R, COLS), F32),
        ),
        in_specs=[
            pl.BlockSpec(memory_space=pltpu.HBM),
            pl.BlockSpec(memory_space=pltpu.HBM),
            whole,
        ],
        out_specs=(whole, whole, whole),
        scratch_shapes=[
            pltpu.VMEM((D, 2 * COLS), BF16),
            pltpu.VMEM((2 * COLS, D), BF16),
            pltpu.VMEM((3 * R, 2 * COLS), BF16),
            pltpu.VMEM((128, PIECE, 128), F32),
            pltpu.VMEM((CHUNKS, 16, PIECE, 128), F32),
            pltpu.VMEM((CHUNKS, 16, PIECE, 128), F32),
            pltpu.VMEM((64, PIECE, 128), F32),
            pltpu.VMEM((128, PIECE, 128), F32),
            pltpu.VMEM((R, COLS), F32),
            pltpu.VMEM((REPL, 8, COLS), F32),
            pltpu.VMEM((R, COLS), F32),
            pltpu.VMEM((R, R), F32),
            dma((CHUNKS, 2)),
            dma((CHUNKS,)),
            dma((CHUNKS,)),
            dma(()),
            dma(()),
            dma(()),
            dma((CHUNKS,)),
            dma((CHUNKS,)),
            dma((CHUNKS,)),
            dma(()),
            dma(()),
            dma(()),
            dma(()),
        ],
        compiler_params=pltpu.CompilerParams(
            collective_id=0, has_side_effects=True, vmem_limit_bytes=VMEM_LIMIT
        ),
    )(gradient, error_in, warm_start)
    return pl.pallas_call(
        finish,
        name="error_feedback",
        grid=(D // BLOCK,),
        out_shape=(
            jax.ShapeDtypeStruct((R, COLS), F32),
            jax.ShapeDtypeStruct((1, D, COLS), BF16),
        ),
        in_specs=[block, block, whole, whole, whole],
        out_specs=(whole, block),
        compiler_params=pltpu.CompilerParams(vmem_limit_bytes=VMEM_LIMIT),
    )(gradient, error_in, left_one, second, right)


def solution(mesh):
    in_specs = (P("dp", None, "tensor"), P("dp", None, "tensor"), P(None, "tensor"))
    out_specs = (P(None, "tensor"), P("dp", None, "tensor"))
    return jax.shard_map(shards, mesh=mesh, in_specs=in_specs, out_specs=out_specs, check_vma=False)
```

```python
import jax
import jax.numpy as jnp
from jax import lax
from jax.experimental import pallas as pl
from jax.experimental.pallas import tpu as pltpu
from jax.sharding import PartitionSpec as P

ITERS = 4
REPL = 8
R = 64
D = 4096
COLS = 896
CHUNKS = 4
ROWS = D // CHUNKS
PIECE = 16
BLOCK = 1024
VMEM_LIMIT = 46 * 1024 * 1024
MESH = pl.DeviceIdType.MESH
F32 = jnp.float32
BF16 = jnp.bfloat16
HIGHEST = lax.Precision.HIGHEST


def hops(step):
    return min(step, 4 - step)


OFFSETS = sorted(
    [(i, j, k) for i in range(4) for j in range(4) for k in range(4) if i + j + k],
    key=lambda o: -sum(map(hops, o)),
)

DP_OFFSETS = ((1, 2), (1, 1), (1, 3), (0, 2), (0, 1), (0, 3), (1, 0))


def terms(value):
    high = value.astype(BF16)
    rest = value - high.astype(F32)
    middle = rest.astype(BF16)
    low = (rest - middle.astype(F32)).astype(BF16)
    return high, middle, low


def sum_terms(product):
    return product[0:R] + product[R : 2 * R] + product[2 * R : 3 * R]


def contract(a, b, dim_a, dim_b, precision=None):
    return lax.dot_general(
        a, b, (((dim_a,), (dim_b,)), ((), ())), precision=precision, preferred_element_type=F32
    )


def inverse_cholesky(gram):
    ahead = 8
    lane = lax.broadcasted_iota(jnp.int32, (R, 2 * R), 1)
    sub = lax.broadcasted_iota(jnp.int32, (R, 2 * R), 0)
    work = jnp.concatenate([gram, jnp.zeros((R, R), F32)], axis=1)
    work = jnp.where(lane == sub + R, 1.0, work)
    for j in range(0, R, ahead):
        cols = [jnp.broadcast_to(work[:, j + k : j + k + 1], (R, 2 * R)) for k in range(ahead)]
        rows = [work[j + k : j + k + 1, :] for k in range(ahead)]
        factors = []
        for k in range(ahead):
            pivot = 1.0 / cols[k][j + k : j + k + 1, :]
            factor = jnp.where(sub > j + k, cols[k] * pivot, 0.0)
            factors.append(factor)
            for m in range(k + 1, ahead):
                cols[m] = cols[m] - factor * cols[m][j + k : j + k + 1, :]
                rows[m] = rows[m] - factor[j + m : j + m + 1, :] * rows[k]
        for k in range(ahead):
            work = work - factors[k] * rows[k]
    diagonal = jnp.sum(jnp.where(lane == sub, work, 0.0), axis=1, keepdims=True)
    return work[:, R:] * lax.rsqrt(diagonal)


def kernel(
    gradient, error, warm, flat, second_out, right_out,
    both, turned, rr, part, cross, mine, slots, left, raw_part, raw_slots, raw, first_sweep,
    load_sem, cross_send, cross_recv, rs_send, rs_recv, ag_send, ag_recv, fwd_send, fwd_recv,
    dp_send, dp_recv, dpg_send, dpg_recv,
):
    d, t = lax.axis_index("dp"), lax.axis_index("tensor")
    x, y, z, c = d % 4, (t // 8) * 2 + d // 4, (t // 2) % 4, t % 2
    other = 1 - c
    group = (x + y + z) % 4
    place = x * 4 + y
    chip = place * 4 + z
    own = group * 32 + c * 16 + place

    xs = [(x + i) % 4 for i in range(4)]
    ys = [(y + i) % 4 for i in range(4)]
    dp_of_y = [(j % 2) * 4 for j in ys]
    tensor_of_y = [(j // 2) * 8 for j in ys]
    tensor_of_z = [((z + i) % 4) * 2 + c for i in range(4)]
    xs_places = [i * 4 for i in xs]
    dp_of_step = [((d // 4 + i) % 2) * 4 for i in range(2)]

    def away(o):
        return (dp_of_y[o[1]] + xs[o[0]], tensor_of_y[o[1]] + tensor_of_z[o[2]])

    sibling = (d, (t // 2) * 2 + other)

    def load(j):
        rows = pl.ds(j * ROWS, ROWS)
        return (
            pltpu.make_async_copy(gradient.at[0, rows], both.at[rows, 0:COLS], load_sem.at[j, 0]),
            pltpu.make_async_copy(error.at[0, rows], both.at[rows, COLS : 2 * COLS], load_sem.at[j, 1]),
        )

    for j in range(CHUNKS):
        for copy in load(j):
            copy.start()

    barrier = pltpu.get_barrier_semaphore()
    for o in OFFSETS:
        pl.semaphore_signal(barrier, 1, device_id=away(o), device_id_type=MESH)
    pl.semaphore_signal(barrier, 1, device_id=sibling, device_id_type=MESH)

    def set_right(value):
        for i, term in enumerate(terms(value)):
            rr[i * R : (i + 1) * R, 0:COLS] = term
            rr[i * R : (i + 1) * R, COLS : 2 * COLS] = term

    set_right(warm[...])

    def remote(src, dst, send, recv, target):
        return pltpu.make_async_remote_copy(src, dst, send, recv, device_id=target, device_id_type=MESH)

    def cross_copy(j):
        return remote(part.at[pl.ds(j * 32 + other * 16, 16)], cross.at[j], cross_send.at[j], cross_recv.at[j], sibling)

    def fwd_copy(j):
        half = left.at[pl.ds(j * 32 + c * 16, 16)]
        return remote(half, half, fwd_send.at[j], fwd_recv.at[j], sibling)

    def keep(j, product):
        product = sum_terms(product)
        for b in range(8):
            part[pl.ds(j * 32 + b * 4, 4)] = product[:, b * 128 : (b + 1) * 128].reshape(4, PIECE, 128)

    def row_chunk(j):
        return pl.ds(pl.multiple_of(j * ROWS, ROWS), ROWS)

    def loaded(j):
        rows = row_chunk(j)
        pltpu.make_async_copy(gradient.at[0, rows], both.at[rows, 0:COLS], load_sem.at[j, 0]).wait()
        pltpu.make_async_copy(error.at[0, rows], both.at[rows, COLS : 2 * COLS], load_sem.at[j, 1]).wait()

    def first_product(j):
        loaded(j)
        keep(j, contract(rr[...], both[row_chunk(j), :], 1, 1))

    def scatter_chunk(j):
        cross_copy(j).wait_recv()
        mine[j] = part[pl.ds(j * 32 + c * 16, 16)] + cross[j]
        def send_from(g):
            @pl.when(group == g)
            def _():
                for o in OFFSETS:
                    if (sum(o) + g - j) % 4 == 0:
                        source = mine.at[j, xs_places[o[0]] + ys[o[1]]]
                        remote(source, slots.at[chip], rs_send, rs_recv, away(o)).start()
                if g == j:
                    slots[chip] = mine[j, place]

        for g in range(4):
            send_from(g)

    def gathered(j):
        @pl.when(j == group)
        def _():
            remote(left.at[0:15], left.at[0:15], ag_send, ag_recv.at[j], sibling).wait_recv()

        @pl.when(j != group)
        def _():
            remote(left.at[0:16], left.at[0:16], ag_send, ag_recv.at[j], sibling).wait_recv()

        fwd_copy(j).start()

    def right_chunk(j, carry):
        @pl.when(j < CHUNKS - 1)
        def _():
            gathered(j + 1)

        fwd_copy(j).wait_recv()
        rows = pl.ds(pl.multiple_of(j * ROWS, ROWS), ROWS)
        blocks = left[pl.ds(j * 32, 32)].reshape(8, R, 128)
        value = jnp.concatenate([blocks[b] for b in range(8)], axis=1)
        flat[:, rows] = value
        stacked = jnp.concatenate(terms(value), axis=0)
        product = sum_terms(contract(stacked, both[rows, :], 1, 0))
        raw_part[...] += product[:, 0:COLS] + product[:, COLS : 2 * COLS]
        return carry

    def dp_device(o):
        return dp_of_step[o[0]] + xs[o[1]]

    def ranks(owner):
        return pl.ds(pl.multiple_of(owner * 8, 8), 8)

    first_product(0)
    pl.semaphore_wait(barrier, len(OFFSETS) + 1)

    def iteration(step, _):
        def left_step(j, carry):
            @pl.when((step == 0) & (j > 0))
            def _():
                first_product(j)

            @pl.when(step > 0)
            def _():
                keep(j, jnp.dot(rr[...], turned[:, row_chunk(j)], preferred_element_type=F32))

            cross_copy(j).start()
            return carry

        lax.fori_loop(0, CHUNKS - 1, left_step, 0)
        scatter_chunk(0)
        lax.fori_loop(CHUNKS - 1, CHUNKS, left_step, 0)
        for j in range(1, CHUNKS):
            scatter_chunk(j)

        @pl.when(step == 0)
        def _():
            def turn(j, carry):
                rows = row_chunk(j)
                turned[:, rows] = both[rows, :].T
                return carry

            lax.fori_loop(0, CHUNKS, turn, 0)

        raw_part[...] = jnp.zeros_like(raw_part)
        remote(slots.at[0:63], slots.at[0:63], rs_send, rs_recv, sibling).wait_recv()
        left[own] = jnp.sum(slots[...], axis=0)
        for o in OFFSETS:
            remote(left.at[own], left.at[own], ag_send, ag_recv.at[group], away(o)).start()

        gathered(0)
        lax.fori_loop(0, CHUNKS, right_chunk, 0)

        for k in DP_OFFSETS:
            owner = dp_device(k)
            remote(raw_part.at[ranks(owner)], raw_slots.at[d], dp_send, dp_recv, (owner, t)).start()
        raw_slots[d] = raw_part[ranks(d)]

        @pl.when(step < ITERS)
        def _():
            first_sweep[...] = inverse_cholesky(contract(flat[...], flat[...], 1, 1, HIGHEST))

        remote(raw_slots.at[0:7], raw_slots.at[0:7], dp_send, dp_recv, sibling).wait_recv()
        raw[ranks(d)] = jnp.sum(raw_slots[...], axis=0)
        for k in DP_OFFSETS:
            remote(raw.at[ranks(d)], raw.at[ranks(d)], dpg_send, dpg_recv, (dp_device(k), t)).start()

        @pl.when(step < ITERS)
        def _():
            first = first_sweep[...]
            left_one = jnp.dot(first, flat[...], precision=HIGHEST, preferred_element_type=F32)
            flat[...] = left_one
            second = inverse_cholesky(contract(left_one, left_one, 1, 1, HIGHEST))
            second_out[...] = second
            first_sweep[...] = jnp.dot(second, first, precision=HIGHEST, preferred_element_type=F32) * (1.0 / REPL)

        for j in range(CHUNKS):
            cross_copy(j).wait_send()
            fwd_copy(j).wait_send()
        remote(slots.at[0:63], slots.at[0:63], rs_send, rs_recv, sibling).wait_send()
        remote(left.at[0:63], left.at[0:63], ag_send, ag_recv.at[0], sibling).wait_send()
        remote(raw_slots.at[0:7], raw_slots.at[0:7], dp_send, dp_recv, sibling).wait_send()
        remote(raw_slots.at[0:7], raw_slots.at[0:7], dpg_send, dpg_recv, sibling).wait()

        right = jnp.dot(first_sweep[...], raw[...], precision=HIGHEST, preferred_element_type=F32)
        right_out[...] = right
        set_right(right)
        return 0

    lax.fori_loop(0, ITERS, iteration, 0)


def finish(gradient, error, left_one, second, right, right_out, error_out):
    @pl.when(pl.program_id(0) == 0)
    def _():
        right_out[...] = right[...]

    high, middle, _ = terms(right[...])
    right_terms = jnp.concatenate([high, high, middle, middle], axis=0)
    rows = pl.ds(pl.multiple_of(pl.program_id(0) * BLOCK, BLOCK), BLOCK)
    basis = jnp.dot(second[...], left_one[:, rows], precision=HIGHEST, preferred_element_type=F32)
    basis_high, basis_middle, _ = terms(basis)
    basis_terms = jnp.concatenate([basis_high, basis_middle, basis_high, basis_middle], axis=0).T
    approx = jnp.dot(basis_terms, right_terms, preferred_element_type=F32)
    merged = gradient[0].astype(F32) + error[0].astype(F32)
    error_out[0] = (merged - approx).astype(BF16)


def shards(gradient, error_in, warm_start):
    dma = pltpu.SemaphoreType.DMA
    block = pl.BlockSpec((1, BLOCK, COLS), lambda i: (0, i, 0))
    whole = pl.BlockSpec(memory_space=pltpu.VMEM)
    left_one, second, right = pl.pallas_call(
        kernel,
        name="power_iterations",
        out_shape=(
            jax.ShapeDtypeStruct((R, D), F32),
            jax.ShapeDtypeStruct((R, R), F32),
            jax.ShapeDtypeStruct((R, COLS), F32),
        ),
        in_specs=[
            pl.BlockSpec(memory_space=pltpu.HBM),
            pl.BlockSpec(memory_space=pltpu.HBM),
            whole,
        ],
        out_specs=(whole, whole, whole),
        scratch_shapes=[
            pltpu.VMEM((D, 2 * COLS), BF16),
            pltpu.VMEM((2 * COLS, D), BF16),
            pltpu.VMEM((3 * R, 2 * COLS), BF16),
            pltpu.VMEM((128, PIECE, 128), F32),
            pltpu.VMEM((CHUNKS, 16, PIECE, 128), F32),
            pltpu.VMEM((CHUNKS, 16, PIECE, 128), F32),
            pltpu.VMEM((64, PIECE, 128), F32),
            pltpu.VMEM((128, PIECE, 128), F32),
            pltpu.VMEM((R, COLS), F32),
            pltpu.VMEM((REPL, 8, COLS), F32),
            pltpu.VMEM((R, COLS), F32),
            pltpu.VMEM((R, R), F32),
            dma((CHUNKS, 2)),
            dma((CHUNKS,)),
            dma((CHUNKS,)),
            dma(()),
            dma(()),
            dma(()),
            dma((CHUNKS,)),
            dma((CHUNKS,)),
            dma((CHUNKS,)),
            dma(()),
            dma(()),
            dma(()),
            dma(()),
        ],
        compiler_params=pltpu.CompilerParams(
            collective_id=0, has_side_effects=True, vmem_limit_bytes=VMEM_LIMIT
        ),
    )(gradient, error_in, warm_start)
    return pl.pallas_call(
        finish,
        name="error_feedback",
        grid=(D // BLOCK,),
        out_shape=(
            jax.ShapeDtypeStruct((R, COLS), F32),
            jax.ShapeDtypeStruct((1, D, COLS), BF16),
        ),
        in_specs=[block, block, whole, whole, whole],
        out_specs=(whole, block),
        compiler_params=pltpu.CompilerParams(vmem_limit_bytes=VMEM_LIMIT),
    )(gradient, error_in, left_one, second, right)


def solution(mesh):
    in_specs = (P("dp", None, "tensor"), P("dp", None, "tensor"), P(None, "tensor"))
    out_specs = (P(None, "tensor"), P("dp", None, "tensor"))
    return jax.shard_map(shards, mesh=mesh, in_specs=in_specs, out_specs=out_specs, check_vma=False)
```
